32 devices in a mesh: stream: 4 (over y, x), tile: 8 (over z, core).
Axes of the slice: x: 2, y: 2, z: 4, core: 2. Of those that a mesh axis runs over, the one named last changes fastest.
Arguments:
- frame_in: bfloat16 [16, 16, 128, 384], P('stream', 'tile'), may hold values from -6 to 6
- cache_first: bfloat16 [16, 2, 16, 128, 384], P('stream', None, 'tile'), may hold values from -6 to 6
- cache_second: bfloat16 [16, 2, 16, 128, 384], P('stream', None, 'tile'), may hold values from -6 to 6
- gain_first: float32 [384], replicated, may hold values from 0.1 to 1.9
- gain_second: float32 [384], replicated, may hold values from 0.1 to 1.9
- conv_first: bfloat16 [3, 3, 3, 384, 384], replicated, may hold values from -0.0625 to 0.0625
- conv_second: bfloat16 [3, 3, 3, 384, 384], replicated, may hold values from -0.0625 to 0.0625
- bias_first: float32 [384], replicated, may hold values from -0.5 to 0.5
- bias_second: float32 [384], replicated, may hold values from -0.5 to 0.5
- old_slot: int32 [16], replicated, may hold values from 0 to 15, as said below
- new_slot: int32 [16], replicated, may hold values from 0 to 15, as said below
- old_shift: int32 [16], replicated, may hold values from 0 to 7
- new_shift: int32 [16], replicated, may hold values from 0 to 7
- frame_count: int32 [16], replicated, may hold values from 0 to 2
Outputs:
- mixed_frame: bfloat16 [16, 16, 128, 384], P('stream', 'tile')
- next_first: bfloat16 [16, 2, 16, 128, 384], P('stream', None, 'tile')
- next_second: bfloat16 [16, 2, 16, 128, 384], P('stream', None, 'tile')
The draws below stay inside these ranges and needn't reach their ends.
Inputs may be any that keep to these rules, and one draw needn't show every extreme that they name: `old_slot`: slot q is position q % 4 of group q // 4; every slot holds one stream. `new_slot`: every slot holds one stream; of the streams of one old group at most 2 go to any one new group, and from every old group exactly 2 go to one same group.
All inputs are finite; a program needn't handle non-finite values.
Results may differ from the reference program's by a relative error of at most 0.0025.
Values may be sent and summed in bfloat16 or wider, within the bound.
A program may use at most 128 MiB of HBM per device.

```python
import jax
import jax.numpy as jnp
from jax import lax

C = 384
SLOTS = 4
ROWS = 2
COLS = 128
CAP = 2
FLIGHT = 16
TILES = 8
HROWS = 16


def slot_plan(key):
    groups = FLIGHT // SLOTS
    old_slots = jax.random.permutation(jax.random.fold_in(key, 11), FLIGHT).astype(jnp.int32)
    group_order = jax.random.permutation(jax.random.fold_in(key, 12), groups).astype(jnp.int32)
    positions_all = jnp.arange(SLOTS, dtype=jnp.int32)
    chosen = jnp.where(positions_all < CAP, 0, 1 + (positions_all - CAP) % max(groups - 1, 1))
    offsets = group_order[chosen]
    places = jax.vmap(lambda group_id: jax.random.permutation(jax.random.fold_in(key, 100 + group_id), SLOTS).astype(jnp.int32))(jnp.arange(groups, dtype=jnp.int32))
    old_group = old_slots // SLOTS
    new_position = places[old_group, old_slots % SLOTS]
    target_group = (old_group + offsets[new_position]) % groups
    new_slots = (target_group * SLOTS + new_position).astype(jnp.int32)
    return (old_slots, new_slots)


def draw_old_slot(key, part):
    return slot_plan(key)[0]


def draw_new_slot(key, part):
    return slot_plan(key)[1]


def touch_ends(entries, rng, smallest, top_value):
    index_at = [jax.random.randint(jax.random.fold_in(rng, axis), (), 0, length) for axis, length in enumerate(entries.shape)]
    main_axis = entries.shape.index(max(entries.shape))
    neighbour = index_at[:main_axis] + [(index_at[main_axis] + 1) % entries.shape[main_axis]] + index_at[main_axis + 1:]
    return entries.at[tuple(index_at)].set(smallest).at[tuple(neighbour)].set(top_value)


def levels(key, shape, cuts, smallest, high):
    def one(axis_at, shards_of):
        steps = jax.random.uniform(jax.random.fold_in(jax.random.fold_in(key, 6), axis_at), (shards_of,), jnp.float32, smallest / len(cuts), high / len(cuts))
        return jnp.repeat(jnp.exp(steps), shape[axis_at] // shards_of).reshape((-1,) + (1,) * (len(shape) - axis_at - 1))

    level = one(*cuts[0])
    for cut in cuts[1:]:
        level = level * one(*cut)
    return level


def scatter_about(rng, shape, width, limit, cuts=(), kind=jnp.bfloat16):
    array = jax.random.normal(rng, shape, jnp.float32) * width
    if len(cuts) > 0:
        array = levels(rng, shape, cuts, -0.22, 0.18) * array
    return jnp.clip(array, min=-limit, max=limit).astype(kind)


def setup_inputs(seed: int = 0) -> dict:
    keys = jax.random.split(jax.random.key(seed), 15)
    return {
        "frame_in": scatter_about(keys[0], (FLIGHT, HROWS, COLS, C), 1.0, 6.0, ((0, 4), (1, 8))),
        "cache_first": scatter_about(keys[1], (FLIGHT, 2, HROWS, COLS, C), 1.0, 6.0, ((0, 4), (2, 8))),
        "cache_second": scatter_about(keys[2], (FLIGHT, 2, HROWS, COLS, C), 1.0, 6.0, ((0, 4), (2, 8))),
        "gain_first": jnp.clip(1.0 + 0.18 * jax.random.normal(keys[3], (C,), jnp.float32), 0.1, 1.9),
        "gain_second": jnp.clip(1.0 + 0.18 * jax.random.normal(keys[4], (C,), jnp.float32), 0.1, 1.9),
        "conv_first": scatter_about(keys[5], (3, 3, 3, C, C), (27 * C) ** -0.5, 0.0625),
        "conv_second": scatter_about(keys[6], (3, 3, 3, C, C), (27 * C) ** -0.5, 0.0625),
        "bias_first": jnp.clip(jax.random.uniform(keys[7], (C,), jnp.float32, -0.5, 0.5), -0.5, 0.5),
        "bias_second": jnp.clip(jax.random.uniform(keys[8], (C,), jnp.float32, -0.5, 0.5), -0.5, 0.5),
        "old_slot": draw_old_slot(jax.random.fold_in(keys[14], 71), 0),
        "new_slot": draw_new_slot(jax.random.fold_in(keys[14], 71), 0),
        "old_shift": touch_ends(jax.random.randint(keys[11], (FLIGHT,), 0, TILES), jax.random.fold_in(keys[11], 1), 0, TILES - 1).astype(jnp.int32),
        "new_shift": touch_ends(jax.random.randint(keys[12], (FLIGHT,), 0, TILES), jax.random.fold_in(keys[12], 1), 0, TILES - 1).astype(jnp.int32),
        "frame_count": touch_ends(jax.random.randint(keys[13], (FLIGHT,), 0, 3), jax.random.fold_in(keys[13], 1), 0, 2).astype(jnp.int32),
    }


def activate(values, gain):
    scaled = values * lax.rsqrt(lax.optimization_barrier(jnp.mean(values * values, axis=-1, keepdims=True)) + 1e-06)
    return jax.nn.silu(scaled * gain)

def convolve(stacked, weight, bias_vec):
    n_rows = stacked.shape[1]
    n_cols = stacked.shape[2]
    channels = stacked.shape[3]
    padded = jnp.pad(stacked, ((0, 0), (1, 1), (1, 1), (0, 0)))
    pieces = [padded[t_step, y_step:y_step + n_rows, x_step:x_step + n_cols, :] for t_step in range(3) for y_step in range(3) for x_step in range(3)]
    patches = jnp.concatenate(pieces, axis=-1).reshape(-1, 27 * channels).astype(jnp.float32)
    kernel = weight.reshape(27 * channels, channels).astype(jnp.float32)
    result = jnp.dot(patches, kernel, preferred_element_type=jnp.float32, precision=lax.Precision.HIGHEST) + bias_vec
    return result.reshape(n_rows, n_cols, channels)

def reference(frame_in, cache_first, cache_second, gain_first, gain_second, conv_first, conv_second, bias_first, bias_second, old_slot, new_slot, old_shift, new_shift, frame_count):
    all_rows = frame_in.shape[1]
    row_ids = jnp.arange(all_rows, dtype=jnp.int32)

    def natural(stored, shift_rows):
        return jnp.take(stored, (row_ids + shift_rows * ROWS) % all_rows, axis=-3)

    def restored(natural_frame, shift_rows):
        return jnp.take(natural_frame, (row_ids - shift_rows * ROWS) % all_rows, axis=-3)

    def per_stream(stream):
        frames_done = frame_count[stream]
        frame_keep = jnp.stack([frames_done >= 2, frames_done >= 1]).astype(jnp.bfloat16)[:, None, None, None]
        prior_first = natural(cache_first[old_slot[stream]], old_shift[stream]) * frame_keep
        prior_second = natural(cache_second[old_slot[stream]], old_shift[stream]) * frame_keep
        current = natural(frame_in[new_slot[stream]], new_shift[stream])
        act_first = activate(current.astype(jnp.float32), gain_first).astype(jnp.bfloat16)
        hidden = convolve(jnp.concatenate([prior_first, act_first[None]], axis=0), conv_first, bias_first)
        act_second = activate(hidden, gain_second).astype(jnp.bfloat16)
        second_out = convolve(jnp.concatenate([prior_second, act_second[None]], axis=0), conv_second, bias_second)
        mixed = (second_out + current.astype(jnp.float32)).astype(jnp.bfloat16)
        shift_new = new_shift[stream]
        next_a = jnp.stack([prior_first[1], act_first], axis=0)
        next_b = jnp.stack([prior_second[1], act_second], axis=0)
        return (restored(mixed, shift_new), restored(next_a, shift_new), restored(next_b, shift_new))
    results = lax.map(per_stream, jnp.arange(FLIGHT, dtype=jnp.int32))
    inverse = jnp.zeros((FLIGHT,), jnp.int32).at[new_slot].set(jnp.arange(FLIGHT, dtype=jnp.int32))
    return (results[0][inverse], results[1][inverse], results[2][inverse])
```

```python
import functools

import jax
import jax.numpy as jnp
from jax import lax
from jax.experimental import pallas as pl
from jax.experimental.pallas import tpu as pltpu
from jax.sharding import PartitionSpec as P

BF16 = jnp.bfloat16
F32 = jnp.float32
VMEM_BYTES = 56 * 1024 * 1024
ANY = pl.BlockSpec(memory_space=pl.ANY)
SMEM = pl.BlockSpec(memory_space=pltpu.SMEM)
LOT_SIZES = (0, 1, 2, 3, 4, 5, 6, 8, 10, 12, 16, 24, 32)
SLOTS_PER_STEP = 2


def exchange_kernel(groups, pick, out_of, *refs):
    n_in = len(refs) - 4
    ins, (out, send_sem, recv_sem, local_sem) = refs[:n_in], refs[n_in:]
    me = lax.axis_index("stream")
    barrier = pltpu.get_barrier_semaphore()
    for peer in range(groups):

        @pl.when(me != peer)
        def _():
            pl.semaphore_signal(
                barrier, inc=1, device_id={"stream": peer}, device_id_type=pl.DeviceIdType.MESH
            )

    pl.semaphore_wait(barrier, groups - 1)

    def remote(peer, source, target, slot):
        return pltpu.make_async_remote_copy(
            src_ref=source,
            dst_ref=target,
            send_sem=send_sem.at[peer],
            recv_sem=recv_sem.at[slot],
            device_id={"stream": peer},
            device_id_type=pl.DeviceIdType.MESH,
        )

    for peer in range(groups):

        @pl.when(me != peer)
        def _():
            remote(peer, pick(ins, peer), out.at[me], me).start()

        @pl.when(me == peer)
        def _():
            pltpu.make_async_copy(pick(ins, peer), out.at[peer], local_sem).start()

    for peer in range(groups):

        @pl.when(me != peer)
        def _():
            remote(peer, pick(ins, peer), out.at[me], me).wait_send()
            remote(peer, out.at[peer], out.at[peer], peer).wait_recv()

        @pl.when(me == peer)
        def _():
            pltpu.make_async_copy(pick(ins, peer), out.at[peer], local_sem).wait()


def exchange(groups, pick, out_shape, collective_id, *arrays):
    return pl.pallas_call(
        functools.partial(exchange_kernel, groups, pick, None),
        out_shape=jax.ShapeDtypeStruct(out_shape, BF16),
        in_specs=[ANY] * len(arrays),
        out_specs=ANY,
        scratch_shapes=[
            pltpu.SemaphoreType.DMA((groups,)),
            pltpu.SemaphoreType.DMA((groups,)),
            pltpu.SemaphoreType.DMA,
        ],
        compiler_params=pltpu.CompilerParams(
            collective_id=collective_id, has_side_effects=True, vmem_limit_bytes=VMEM_BYTES
        ),
    )(*arrays)


def gather_kernel(count, index_ref, source, out, sems):
    def copy(i):
        return pltpu.make_async_copy(source.at[index_ref[i]], out.at[i], sems.at[i])

    for i in range(count):
        copy(i).start()
    for i in range(count):
        copy(i).wait()


def gather_items(source, index):
    count = index.shape[0]
    return pl.pallas_call(
        functools.partial(gather_kernel, count),
        out_shape=jax.ShapeDtypeStruct((count,) + source.shape[1:], source.dtype),
        in_specs=[SMEM, ANY],
        out_specs=ANY,
        scratch_shapes=[pltpu.SemaphoreType.DMA((count,))],
        compiler_params=pltpu.CompilerParams(vmem_limit_bytes=VMEM_BYTES),
    )(index, source)


def load_weights(w_ref, w_s, sems, channels):
    copies = []
    for t in range(3):
        for dy in range(3):
            for dx in range(3):
                copies.append(
                    pltpu.make_async_copy(
                        w_ref.at[t, dy, dx],
                        w_s.at[
                            pl.ds(t * channels, channels),
                            pl.ds((dy * 3 + dx) * channels, channels),
                        ],
                        sems.at[t * 9 + dy * 3 + dx],
                    )
                )
    for copy in copies:
        copy.start()
    for copy in copies:
        copy.wait()


def activate(values, gain):
    scaled = values * lax.rsqrt(jnp.mean(values * values, axis=-1, keepdims=True) + 1e-06)
    u = scaled * gain
    return u / (1.0 + jnp.exp(-u))


def conv_rows(x, w_s, cols, channels):
    r = jnp.dot(x, w_s[...], preferred_element_type=F32)
    rows = x.shape[0]
    col = lax.broadcasted_iota(jnp.int32, (rows, channels), 0) % cols
    sums = []
    for dy in range(3):
        part = [
            r[:, (dy * 3 + dx) * channels : (dy * 3 + dx + 1) * channels] for dx in range(3)
        ]
        left = jnp.where(col == 0, 0.0, pltpu.roll(part[0], 1, 0))
        right = jnp.where(col == cols - 1, 0.0, pltpu.roll(part[2], rows - 1, 0))
        sums.append((part[1] + left + right).reshape(-1, 2, cols, channels))
    return sums


def stack_times(count_ref, first_slot, kept, act):
    rows_out = []
    newer = []
    for s in range(act.shape[0]):
        done = count_ref[first_slot + s]
        older_on = done >= 2
        newer_on = done >= 1
        for y in range(2):
            old = kept[y, s, 0]
            new = kept[y, s, 1]
            old = jnp.where(older_on, old, jnp.zeros_like(old))
            new = jnp.where(newer_on, new, jnp.zeros_like(new))
            newer.append((s, y, new))
            rows_out.append(jnp.concatenate([old, new, act[s, y]], axis=-1))
    return jnp.concatenate(rows_out, axis=0), newer


def write_layer(sums, newer, act, part_ref, edge_ref, next_ref, extra):
    below, same, above = sums[0], sums[1], sums[2]
    part_ref[:, 0] = same[:, 0] + above[:, 1] + extra[:, 0]
    part_ref[:, 1] = same[:, 1] + below[:, 0] + extra[:, 1]
    edge_ref[0] = above[:, 0].astype(BF16)
    edge_ref[1] = below[:, 1].astype(BF16)
    for s, y, new in newer:
        next_ref[s, 0, y] = new
    next_ref[:, 1] = act


def first_kernel(
    cols, channels, count_ref, frame_ref, kept_ref, gain_ref, bias_ref, w_ref,
    part_ref, edge_ref, next_ref, w_s, sems,
):
    step = pl.program_id(0)

    @pl.when(step == 0)
    def _():
        load_weights(w_ref, w_s, sems, channels)

    act = activate(frame_ref[...].astype(F32), gain_ref[...]).astype(BF16)
    x, newer = stack_times(count_ref, step * act.shape[0], kept_ref[...], act)
    sums = conv_rows(x, w_s, cols, channels)
    extra = jnp.broadcast_to(bias_ref[...], act.shape)
    write_layer(sums, newer, act, part_ref, edge_ref, next_ref, extra)


def second_kernel(
    cols, channels, count_ref, up_ref, down_ref, frame_ref, kept_ref, gain_ref, bias_ref,
    hidden_ref, got_above_ref, got_below_ref, w_ref, part_ref, edge_ref, next_ref, w_s, sems,
):
    step = pl.program_id(0)

    @pl.when(step == 0)
    def _():
        load_weights(w_ref, w_s, sems, channels)

    slots = hidden_ref.shape[0]
    acts = []
    for s in range(slots):
        here = step * slots + s
        above = got_above_ref[s].astype(F32)
        below = got_below_ref[s].astype(F32)
        above = jnp.where(up_ref[here] > 0, above, 0.0)
        below = jnp.where(down_ref[here] > 0, below, 0.0)
        hidden = jnp.stack([hidden_ref[s, 0] + above, hidden_ref[s, 1] + below])
        acts.append(activate(hidden, gain_ref[...]).astype(BF16))
    act = jnp.stack(acts)
    x, newer = stack_times(count_ref, step * slots, kept_ref[...], act)
    sums = conv_rows(x, w_s, cols, channels)
    extra = frame_ref[...].astype(F32) + bias_ref[...]
    write_layer(sums, newer, act, part_ref, edge_ref, next_ref, extra)


def layer_specs(layer, n_slots, cols, channels):
    step = SLOTS_PER_STEP
    frame = pl.BlockSpec((step, 2, cols, channels), lambda i: (i, 0, 0, 0))
    kept = pl.BlockSpec(
        (2, step, 2, cols, channels), lambda i, layer=layer: (layer, i, 0, 0, 0)
    )
    vector = pl.BlockSpec((1, channels), lambda i: (0, 0))
    edge = pl.BlockSpec((step, cols, channels), lambda i: (i, 0, 0))
    outs = [
        pl.BlockSpec((step, 2, cols, channels), lambda i: (i, 0, 0, 0)),
        pl.BlockSpec((2, step, cols, channels), lambda i: (0, i, 0, 0)),
        pl.BlockSpec((step, 2, 2, cols, channels), lambda i: (i, 0, 0, 0, 0)),
    ]
    shapes = [
        jax.ShapeDtypeStruct((n_slots, 2, cols, channels), F32),
        jax.ShapeDtypeStruct((2, n_slots, cols, channels), BF16),
        jax.ShapeDtypeStruct((n_slots, 2, 2, cols, channels), BF16),
    ]
    scratch = [
        pltpu.VMEM((3 * channels, 9 * channels), BF16),
        pltpu.SemaphoreType.DMA((27,)),
    ]
    return frame, kept, vector, edge, outs, shapes, scratch


def layer_call(kernel, in_specs, outs, shapes, scratch, n_slots, cols, channels, args):
    flops = 2 * n_slots * 2 * cols * 27 * channels * channels
    return pl.pallas_call(
        functools.partial(kernel, cols, channels),
        grid=(n_slots // SLOTS_PER_STEP,),
        in_specs=in_specs,
        out_specs=outs,
        out_shape=shapes,
        scratch_shapes=scratch,
        compiler_params=pltpu.CompilerParams(
            dimension_semantics=("arbitrary",), vmem_limit_bytes=VMEM_BYTES
        ),
        cost_estimate=pl.CostEstimate(
            flops=flops, bytes_accessed=27 * channels * channels * 2 + 8 * 2**20, transcendentals=0
        ),
    )(*args)


def trade_edges(edges):
    n = lax.axis_size("tile")
    from_below = lax.ppermute(edges[0], "tile", [((i + 1) % n, i) for i in range(n)])
    from_above = lax.ppermute(edges[1], "tile", [(i, (i + 1) % n) for i in range(n)])
    return from_above, from_below


def rotate_lots(buffer, starts, counts, places, scale):
    n = lax.axis_size("tile")
    for digit in range(1, places):
        by = digit * scale
        start, count = starts[digit], counts[digit]
        pairs = [(i, (i + by) % n) for i in range(n)]

        def branch(size, buffer, start, count, pairs=pairs):
            if size == 0:
                return buffer
            lot = lax.dynamic_slice_in_dim(buffer, start, size, axis=0)
            moved = lax.ppermute(lot, "tile", pairs)
            taken = jnp.arange(size, dtype=jnp.int32) < count
            lot = jnp.where(taken[:, None, None], moved, lot)
            return lax.dynamic_update_slice_in_dim(buffer, lot, start, axis=0)

        which = sum((count > size).astype(jnp.int32) for size in LOT_SIZES[:-1])
        buffer = lax.switch(
            which, [functools.partial(branch, size) for size in LOT_SIZES], buffer, start, count
        )
    return buffer


def lookup(held_table, values):
    return jnp.sum(jnp.where(held_table, values[None, :], 0), axis=1)


def local(
    frame_in,
    cache_first,
    cache_second,
    gain_first,
    gain_second,
    conv_first,
    conv_second,
    bias_first,
    bias_second,
    old_slot,
    new_slot,
    old_shift,
    new_shift,
    frame_count,
):
    n_slots, n_rows, cols, channels = frame_in.shape
    groups = lax.axis_size("stream")
    n_tiles = lax.axis_size("tile")
    my_group = lax.axis_index("stream")
    my_tile = lax.axis_index("tile")
    flight = old_slot.shape[0]
    ids = jnp.arange(flight, dtype=jnp.int32)
    held_old = old_slot[None, :] == ids[:, None]
    held_new = new_slot[None, :] == ids[:, None]
    turn = (new_shift - old_shift) % n_tiles
    item_turn = lookup(held_old, turn)
    item_done = lookup(held_old, frame_count)
    live = jnp.stack([item_done >= 2, item_done >= 1], axis=1).reshape(-1)
    item_turn = jnp.where(live, jnp.repeat(item_turn, 2), 0)
    n_items = 2 * flight
    room = n_items + 8
    item_ids = jnp.arange(n_items, dtype=jnp.int32)
    room_ids = jnp.arange(room, dtype=jnp.int32)

    block_shape = (groups, n_slots, 2, cols, channels)
    gathered = exchange(
        groups,
        lambda ins, peer: ins[peer // 2].at[:, :, peer % 2],
        block_shape,
        0,
        cache_first,
        cache_second,
    )
    buffer = gathered.reshape((n_items, cols, channels))
    position = item_ids
    scale = 1
    while scale < n_tiles:
        places = min(8, n_tiles // scale)
        digit = item_turn // scale % places
        rank_key = jnp.where(digit == 0, places, digit)
        ahead = (rank_key[None, :] < rank_key[:, None]) | (
            (rank_key[None, :] == rank_key[:, None]) & (item_ids[None, :] < item_ids[:, None])
        )
        new_position = jnp.sum(ahead.astype(jnp.int32), axis=1)
        digits = jnp.arange(places, dtype=jnp.int32)
        counts = jnp.sum((digit[None, :] == digits[:, None]).astype(jnp.int32), axis=1)
        before = (rank_key[None, :] < digits[:, None]).astype(jnp.int32)
        starts = jnp.sum(before, axis=1)
        index = jnp.sum(
            jnp.where(new_position[None, :] == room_ids[:, None], position[None, :], 0), axis=1
        )
        buffer = gather_items(buffer, index)
        buffer = rotate_lots(buffer, starts, counts, places, scale)
        position = new_position
        scale *= places

    origin = lookup(held_new, old_slot)
    wanted = (origin[:, None] * 2 + jnp.arange(2, dtype=jnp.int32)[None, :]).reshape(-1)
    final = jnp.sum(
        jnp.where(wanted[:, None] == item_ids[None, :], position[None, :], 0), axis=1
    )
    outgoing = gather_items(buffer, final).reshape(block_shape)
    kept = exchange(groups, lambda ins, peer: ins[0].at[peer], block_shape, 1, outgoing)

    begin = my_group * n_slots
    my_count = lax.dynamic_slice_in_dim(lookup(held_new, frame_count), begin, n_slots)
    my_shift = lax.dynamic_slice_in_dim(lookup(held_new, new_shift), begin, n_slots)
    number = (my_tile - my_shift) % n_tiles
    has_above = (number != 0).astype(jnp.int32)
    has_below = (number != n_tiles - 1).astype(jnp.int32)

    gain_first, gain_second = gain_first.reshape(1, -1), gain_second.reshape(1, -1)
    bias_first, bias_second = bias_first.reshape(1, -1), bias_second.reshape(1, -1)
    frame, kept_spec, vector, edge, outs, shapes, scratch = layer_specs(0, n_slots, cols, channels)
    hidden, edges, next_first = layer_call(
        first_kernel,
        [SMEM, frame, kept_spec, vector, vector, ANY],
        outs, shapes, scratch, n_slots, cols, channels,
        (my_count, frame_in, kept, gain_first, bias_first, conv_first),
    )
    from_above, from_below = trade_edges(edges)
    frame, kept_spec, vector, edge, outs, shapes, scratch = layer_specs(1, n_slots, cols, channels)
    second, edges, next_second = layer_call(
        second_kernel,
        [SMEM, SMEM, SMEM, frame, kept_spec, vector, vector, frame, edge, edge, ANY],
        outs, shapes, scratch, n_slots, cols, channels,
        (
            my_count, has_above, has_below, frame_in, kept, gain_second, bias_second,
            hidden, from_above, from_below, conv_second,
        ),
    )
    from_above, from_below = trade_edges(edges)
    above_on = has_above[:, None, None] > 0
    below_on = has_below[:, None, None] > 0
    mixed_frame = jnp.stack(
        [
            second[:, 0] + jnp.where(above_on, from_above.astype(F32), 0.0),
            second[:, 1] + jnp.where(below_on, from_below.astype(F32), 0.0),
        ],
        axis=1,
    ).astype(BF16)
    return (mixed_frame, next_first, next_second)


def solution(mesh):
    whole = (
        P("stream", "tile", None, None),
        P("stream", None, "tile", None, None),
        P("stream", None, "tile", None, None),
    )
    return jax.shard_map(
        local,
        mesh=mesh,
        in_specs=whole + (P(),) * 11,
        out_specs=whole,
        check_vma=False,
    )
```

```python
import functools

import jax
import jax.numpy as jnp
from jax import lax
from jax.experimental import pallas as pl
from jax.experimental.pallas import tpu as pltpu
from jax.sharding import PartitionSpec as P

BF16 = jnp.bfloat16
F32 = jnp.float32
VMEM_BYTES = 56 * 1024 * 1024
ANY = pl.BlockSpec(memory_space=pl.ANY)
SMEM = pl.BlockSpec(memory_space=pltpu.SMEM)
VMEM = pl.BlockSpec(memory_space=pltpu.VMEM)
LOT_SIZES = (0, 2, 4, 6, 10, 32)
SLOTS_PER_STEP = 2


def greet_peers(groups, me):
    barrier = pltpu.get_barrier_semaphore()
    for peer in range(groups):

        @pl.when(me != peer)
        def _():
            pl.semaphore_signal(
                barrier, inc=1, device_id={"stream": peer}, device_id_type=pl.DeviceIdType.MESH
            )

    pl.semaphore_wait(barrier, groups - 1)


def remote_copy(peer, source, target, send_sem, recv_sem):
    return pltpu.make_async_remote_copy(
        src_ref=source,
        dst_ref=target,
        send_sem=send_sem,
        recv_sem=recv_sem,
        device_id={"stream": peer},
        device_id_type=pl.DeviceIdType.MESH,
    )


def item_place(i, n_slots):
    return lax.div(i, 2 * n_slots), lax.rem(lax.div(i, 2), n_slots), lax.rem(i, 2)


def spread_kernel(
    groups, n_slots, index_ref, first_ref, second_ref, out_ref, held, send_sem, recv_sem, local_sem
):
    me = lax.axis_index("stream")
    greet_peers(groups, me)
    caches = (first_ref, second_ref)

    def part(peer):
        return caches[peer // 2].at[:, :, peer % 2]

    for peer in range(groups):

        @pl.when(me != peer)
        def _():
            remote_copy(
                peer, part(peer), held.at[me], send_sem.at[peer], recv_sem.at[me]
            ).start()

        @pl.when(me == peer)
        def _():
            pltpu.make_async_copy(part(peer), held.at[peer], local_sem).start()

    for peer in range(groups):

        @pl.when(me != peer)
        def _():
            remote_copy(
                peer, part(peer), held.at[me], send_sem.at[peer], recv_sem.at[me]
            ).wait_send()
            remote_copy(
                peer, held.at[peer], held.at[peer], send_sem.at[peer], recv_sem.at[peer]
            ).wait_recv()

        @pl.when(me == peer)
        def _():
            pltpu.make_async_copy(part(peer), held.at[peer], local_sem).wait()

    def place(j, carry):
        group, slot, frame = item_place(index_ref[j], n_slots)
        out_ref[j] = held[group, slot, frame]
        return carry

    lax.fori_loop(0, out_ref.shape[0], place, 0)


def collect_kernel(
    groups, n_slots, index_ref, items_ref, out_ref, staged, send_sem, recv_sem, local_sem
):
    me = lax.axis_index("stream")
    greet_peers(groups, me)
    per_group = 2 * n_slots

    for peer in range(groups):

        def place(j, carry):
            group, slot, frame = item_place(j, n_slots)
            staged[group, slot, frame] = items_ref[index_ref[j]]
            return carry

        lax.fori_loop(peer * per_group, (peer + 1) * per_group, place, 0)

        @pl.when(me != peer)
        def _():
            remote_copy(
                peer, staged.at[peer], out_ref.at[me], send_sem.at[peer], recv_sem.at[me]
            ).start()

        @pl.when(me == peer)
        def _():
            pltpu.make_async_copy(staged.at[peer], out_ref.at[peer], local_sem).start()

    for peer in range(groups):

        @pl.when(me != peer)
        def _():
            remote_copy(
                peer, staged.at[peer], out_ref.at[me], send_sem.at[peer], recv_sem.at[me]
            ).wait_send()
            remote_copy(
                peer, out_ref.at[peer], out_ref.at[peer], send_sem.at[peer], recv_sem.at[peer]
            ).wait_recv()

        @pl.when(me == peer)
        def _():
            pltpu.make_async_copy(staged.at[peer], out_ref.at[peer], local_sem).wait()


def exchange(kernel, in_specs, out_spec, out_shape, block_shape, collective_id, args):
    groups, n_slots = block_shape[:2]
    return pl.pallas_call(
        functools.partial(kernel, groups, n_slots),
        out_shape=jax.ShapeDtypeStruct(out_shape, BF16),
        in_specs=in_specs,
        out_specs=out_spec,
        scratch_shapes=[
            pltpu.VMEM(block_shape, BF16),
            pltpu.SemaphoreType.DMA((groups,)),
            pltpu.SemaphoreType.DMA((groups,)),
            pltpu.SemaphoreType.DMA,
        ],
        compiler_params=pltpu.CompilerParams(
            collective_id=collective_id, has_side_effects=True, vmem_limit_bytes=VMEM_BYTES
        ),
    )(*args)


def gather_kernel(index_ref, source, out):
    def place(j, carry):
        out[j] = source[index_ref[j]]
        return carry

    lax.fori_loop(0, out.shape[0], place, 0)


def gather_items(source, index):
    return pl.pallas_call(
        gather_kernel,
        out_shape=jax.ShapeDtypeStruct(index.shape + source.shape[1:], source.dtype),
        in_specs=[SMEM, VMEM],
        out_specs=VMEM,
        compiler_params=pltpu.CompilerParams(vmem_limit_bytes=VMEM_BYTES),
    )(index, source)


def load_weights(w_ref, w_s, sems, channels):
    copies = []
    for t in range(3):
        for dy in range(3):
            for dx in range(3):
                copies.append(
                    pltpu.make_async_copy(
                        w_ref.at[t, dy, dx],
                        w_s.at[
                            pl.ds(t * channels, channels),
                            pl.ds((dy * 3 + dx) * channels, channels),
                        ],
                        sems.at[t * 9 + dy * 3 + dx],
                    )
                )
    for copy in copies:
        copy.start()
    for copy in copies:
        copy.wait()


def activate(values, gain):
    scaled = values * lax.rsqrt(jnp.mean(values * values, axis=-1, keepdims=True) + 1e-06)
    u = scaled * gain
    return u / (1.0 + jnp.exp(-u))


def conv_rows(x, w_s, cols, channels):
    r = jnp.dot(x, w_s[...], preferred_element_type=F32)
    rows = x.shape[0]
    col = lax.broadcasted_iota(jnp.int32, (rows, channels), 0) % cols
    sums = []
    for dy in range(3):
        part = [
            r[:, (dy * 3 + dx) * channels : (dy * 3 + dx + 1) * channels] for dx in range(3)
        ]
        left = jnp.where(col == 0, 0.0, pltpu.roll(part[0], 1, 0))
        right = jnp.where(col == cols - 1, 0.0, pltpu.roll(part[2], rows - 1, 0))
        sums.append((part[1] + left + right).reshape(-1, 2, cols, channels))
    return sums


def stack_times(count_ref, first_slot, kept, act):
    rows_out = []
    newer = []
    for s in range(act.shape[0]):
        done = count_ref[first_slot + s]
        older_on = done >= 2
        newer_on = done >= 1
        for y in range(2):
            old = kept[y, s, 0]
            new = kept[y, s, 1]
            old = jnp.where(older_on, old, jnp.zeros_like(old))
            new = jnp.where(newer_on, new, jnp.zeros_like(new))
            newer.append((s, y, new))
            rows_out.append(jnp.concatenate([old, new, act[s, y]], axis=-1))
    return jnp.concatenate(rows_out, axis=0), newer


def write_layer(sums, newer, act, part_ref, edge_ref, next_ref, extra):
    below, same, above = sums[0], sums[1], sums[2]
    part_ref[:, 0] = same[:, 0] + above[:, 1] + extra[:, 0]
    part_ref[:, 1] = same[:, 1] + below[:, 0] + extra[:, 1]
    edge_ref[0] = above[:, 0].astype(BF16)
    edge_ref[1] = below[:, 1].astype(BF16)
    for s, y, new in newer:
        next_ref[s, 0, y] = new
    next_ref[:, 1] = act


def first_kernel(
    cols, channels, count_ref, frame_ref, kept_ref, gain_ref, bias_ref, w_ref,
    part_ref, edge_ref, next_ref, w_s, sems,
):
    step = pl.program_id(0)

    @pl.when(step == 0)
    def _():
        load_weights(w_ref, w_s, sems, channels)

    act = activate(frame_ref[...].astype(F32), gain_ref[...]).astype(BF16)
    x, newer = stack_times(count_ref, step * act.shape[0], kept_ref[...], act)
    sums = conv_rows(x, w_s, cols, channels)
    extra = jnp.broadcast_to(bias_ref[...], act.shape)
    write_layer(sums, newer, act, part_ref, edge_ref, next_ref, extra)


def second_kernel(
    cols, channels, count_ref, up_ref, down_ref, frame_ref, kept_ref, gain_ref, bias_ref,
    hidden_ref, got_above_ref, got_below_ref, w_ref, part_ref, edge_ref, next_ref, w_s, sems,
):
    step = pl.program_id(0)

    @pl.when(step == 0)
    def _():
        load_weights(w_ref, w_s, sems, channels)

    slots = hidden_ref.shape[0]
    acts = []
    for s in range(slots):
        here = step * slots + s
        above = got_above_ref[s].astype(F32)
        below = got_below_ref[s].astype(F32)
        above = jnp.where(up_ref[here] > 0, above, 0.0)
        below = jnp.where(down_ref[here] > 0, below, 0.0)
        hidden = jnp.stack([hidden_ref[s, 0] + above, hidden_ref[s, 1] + below])
        acts.append(activate(hidden, gain_ref[...]).astype(BF16))
    act = jnp.stack(acts)
    x, newer = stack_times(count_ref, step * slots, kept_ref[...], act)
    sums = conv_rows(x, w_s, cols, channels)
    extra = frame_ref[...].astype(F32) + bias_ref[...]
    write_layer(sums, newer, act, part_ref, edge_ref, next_ref, extra)


def layer_specs(layer, n_slots, cols, channels):
    step = SLOTS_PER_STEP
    frame = pl.BlockSpec((step, 2, cols, channels), lambda i: (i, 0, 0, 0))
    kept = pl.BlockSpec(
        (2, step, 2, cols, channels), lambda i, layer=layer: (layer, i, 0, 0, 0)
    )
    vector = pl.BlockSpec((1, channels), lambda i: (0, 0))
    edge = pl.BlockSpec((step, cols, channels), lambda i: (i, 0, 0))
    outs = [
        pl.BlockSpec((step, 2, cols, channels), lambda i: (i, 0, 0, 0)),
        pl.BlockSpec((2, step, cols, channels), lambda i: (0, i, 0, 0)),
        pl.BlockSpec((step, 2, 2, cols, channels), lambda i: (i, 0, 0, 0, 0)),
    ]
    shapes = [
        jax.ShapeDtypeStruct((n_slots, 2, cols, channels), F32),
        jax.ShapeDtypeStruct((2, n_slots, cols, channels), BF16),
        jax.ShapeDtypeStruct((n_slots, 2, 2, cols, channels), BF16),
    ]
    scratch = [
        pltpu.VMEM((3 * channels, 9 * channels), BF16),
        pltpu.SemaphoreType.DMA((27,)),
    ]
    return frame, kept, vector, edge, outs, shapes, scratch


def layer_call(kernel, in_specs, outs, shapes, scratch, n_slots, cols, channels, args):
    flops = 2 * n_slots * 2 * cols * 27 * channels * channels
    return pl.pallas_call(
        functools.partial(kernel, cols, channels),
        grid=(n_slots // SLOTS_PER_STEP,),
        in_specs=in_specs,
        out_specs=outs,
        out_shape=shapes,
        scratch_shapes=scratch,
        compiler_params=pltpu.CompilerParams(
            dimension_semantics=("arbitrary",), vmem_limit_bytes=VMEM_BYTES
        ),
        cost_estimate=pl.CostEstimate(
            flops=flops, bytes_accessed=27 * channels * channels * 2 + 8 * 2**20, transcendentals=0
        ),
    )(*args)


def trade_edges(edges):
    n = lax.axis_size("tile")
    from_below = lax.ppermute(edges[0], "tile", [((i + 1) % n, i) for i in range(n)])
    from_above = lax.ppermute(edges[1], "tile", [(i, (i + 1) % n) for i in range(n)])
    return from_above, from_below


def rotate_lots(buffer, starts, counts, places, scale):
    n = lax.axis_size("tile")
    for digit in range(1, places):
        by = digit * scale
        start, count = starts[digit], counts[digit]
        pairs = [(i, (i + by) % n) for i in range(n)]

        def branch(size, buffer, start, count, pairs=pairs):
            if size == 0:
                return buffer
            lot = lax.dynamic_slice_in_dim(buffer, start, size, axis=0)
            moved = lax.ppermute(lot, "tile", pairs)
            taken = jnp.arange(size, dtype=jnp.int32) < count
            lot = jnp.where(taken[:, None, None], moved, lot)
            return lax.dynamic_update_slice_in_dim(buffer, lot, start, axis=0)

        which = sum((count > size).astype(jnp.int32) for size in LOT_SIZES[:-1])
        buffer = lax.switch(
            which, [functools.partial(branch, size) for size in LOT_SIZES], buffer, start, count
        )
    return buffer


def lookup(held_table, values):
    return jnp.sum(jnp.where(held_table, values[None, :], 0), axis=1)


def local(
    frame_in,
    cache_first,
    cache_second,
    gain_first,
    gain_second,
    conv_first,
    conv_second,
    bias_first,
    bias_second,
    old_slot,
    new_slot,
    old_shift,
    new_shift,
    frame_count,
):
    n_slots, n_rows, cols, channels = frame_in.shape
    groups = lax.axis_size("stream")
    n_tiles = lax.axis_size("tile")
    my_group = lax.axis_index("stream")
    my_tile = lax.axis_index("tile")
    flight = old_slot.shape[0]
    ids = jnp.arange(flight, dtype=jnp.int32)
    held_old = old_slot[None, :] == ids[:, None]
    held_new = new_slot[None, :] == ids[:, None]
    turn = (new_shift - old_shift) % n_tiles
    item_turn = lookup(held_old, turn)
    item_done = lookup(held_old, frame_count)
    live = jnp.stack([item_done >= 2, item_done >= 1], axis=1).reshape(-1)
    item_turn = jnp.where(live, jnp.repeat(item_turn, 2), 0)
    n_items = 2 * flight
    room = n_items + 24
    item_ids = jnp.arange(n_items, dtype=jnp.int32)
    room_ids = jnp.arange(room, dtype=jnp.int32)

    block_shape = (groups, n_slots, 2, cols, channels)
    buffer = None
    position = item_ids
    scale = 1
    while scale < n_tiles:
        places = min(8, n_tiles // scale)
        digit = item_turn // scale % places
        rank_key = jnp.where(digit == 0, places, digit)
        ahead = (rank_key[None, :] < rank_key[:, None]) | (
            (rank_key[None, :] == rank_key[:, None]) & (item_ids[None, :] < item_ids[:, None])
        )
        new_position = jnp.sum(ahead.astype(jnp.int32), axis=1)
        digits = jnp.arange(places, dtype=jnp.int32)
        counts = jnp.sum((digit[None, :] == digits[:, None]).astype(jnp.int32), axis=1)
        before = (rank_key[None, :] < digits[:, None]).astype(jnp.int32)
        starts = jnp.sum(before, axis=1)
        index = jnp.sum(
            jnp.where(new_position[None, :] == room_ids[:, None], position[None, :], 0), axis=1
        )
        if buffer is None:
            buffer = exchange(
                spread_kernel,
                [SMEM, ANY, ANY],
                VMEM,
                (room, cols, channels),
                block_shape,
                0,
                (index, cache_first, cache_second),
            )
        else:
            buffer = gather_items(buffer, index)
        buffer = rotate_lots(buffer, starts, counts, places, scale)
        position = new_position
        scale *= places

    origin = lookup(held_new, old_slot)
    wanted = (origin[:, None] * 2 + jnp.arange(2, dtype=jnp.int32)[None, :]).reshape(-1)
    final = jnp.sum(
        jnp.where(wanted[:, None] == item_ids[None, :], position[None, :], 0), axis=1
    )
    kept = exchange(
        collect_kernel, [SMEM, VMEM], ANY, block_shape, block_shape, 1, (final, buffer)
    )

    begin = my_group * n_slots
    my_count = lax.dynamic_slice_in_dim(lookup(held_new, frame_count), begin, n_slots)
    my_shift = lax.dynamic_slice_in_dim(lookup(held_new, new_shift), begin, n_slots)
    number = (my_tile - my_shift) % n_tiles
    has_above = (number != 0).astype(jnp.int32)
    has_below = (number != n_tiles - 1).astype(jnp.int32)

    gain_first, gain_second = gain_first.reshape(1, -1), gain_second.reshape(1, -1)
    bias_first, bias_second = bias_first.reshape(1, -1), bias_second.reshape(1, -1)
    frame, kept_spec, vector, edge, outs, shapes, scratch = layer_specs(0, n_slots, cols, channels)
    hidden, edges, next_first = layer_call(
        first_kernel,
        [SMEM, frame, kept_spec, vector, vector, ANY],
        outs, shapes, scratch, n_slots, cols, channels,
        (my_count, frame_in, kept, gain_first, bias_first, conv_first),
    )
    from_above, from_below = trade_edges(edges)
    frame, kept_spec, vector, edge, outs, shapes, scratch = layer_specs(1, n_slots, cols, channels)
    second, edges, next_second = layer_call(
        second_kernel,
        [SMEM, SMEM, SMEM, frame, kept_spec, vector, vector, frame, edge, edge, ANY],
        outs, shapes, scratch, n_slots, cols, channels,
        (
            my_count, has_above, has_below, frame_in, kept, gain_second, bias_second,
            hidden, from_above, from_below, conv_second,
        ),
    )
    from_above, from_below = trade_edges(edges)
    above_on = has_above[:, None, None] > 0
    below_on = has_below[:, None, None] > 0
    mixed_frame = jnp.stack(
        [
            second[:, 0] + jnp.where(above_on, from_above.astype(F32), 0.0),
            second[:, 1] + jnp.where(below_on, from_below.astype(F32), 0.0),
        ],
        axis=1,
    ).astype(BF16)
    return (mixed_frame, next_first, next_second)


def solution(mesh):
    whole = (
        P("stream", "tile", None, None),
        P("stream", None, "tile", None, None),
        P("stream", None, "tile", None, None),
    )
    return jax.shard_map(
        local,
        mesh=mesh,
        in_specs=whole + (P(),) * 11,
        out_specs=whole,
        check_vma=False,
    )
```

```python
import functools

import jax
import jax.numpy as jnp
from jax import lax
from jax.experimental import pallas as pl
from jax.experimental.pallas import tpu as pltpu
from jax.sharding import PartitionSpec as P

BF16 = jnp.bfloat16
F32 = jnp.float32
VMEM_BYTES = 56 * 1024 * 1024
ANY = pl.BlockSpec(memory_space=pl.ANY)
SMEM = pl.BlockSpec(memory_space=pltpu.SMEM)
VMEM = pl.BlockSpec(memory_space=pltpu.VMEM)
LOT_SIZES = (0, 2, 4, 6, 8, 12, 32)
SLOTS_PER_STEP = 2


def greet_peers(groups, me):
    barrier = pltpu.get_barrier_semaphore()
    for peer in range(groups):

        @pl.when(me != peer)
        def _():
            pl.semaphore_signal(
                barrier, inc=1, device_id={"stream": peer}, device_id_type=pl.DeviceIdType.MESH
            )

    pl.semaphore_wait(barrier, groups - 1)


def remote_copy(peer, source, target, send_sem, recv_sem):
    return pltpu.make_async_remote_copy(
        src_ref=source,
        dst_ref=target,
        send_sem=send_sem,
        recv_sem=recv_sem,
        device_id={"stream": peer},
        device_id_type=pl.DeviceIdType.MESH,
    )


def item_place(i, n_slots):
    return lax.div(i, 2 * n_slots), lax.rem(lax.div(i, 2), n_slots), lax.rem(i, 2)


def spread_kernel(
    groups, n_slots, index_ref, first_ref, second_ref, out_ref, held, send_sem, recv_sem, local_sem
):
    me = lax.axis_index("stream")
    greet_peers(groups, me)
    caches = (first_ref, second_ref)

    def part(peer):
        return caches[peer // 2].at[:, :, peer % 2]

    for peer in range(groups):

        @pl.when(me != peer)
        def _():
            remote_copy(
                peer, part(peer), held.at[me], send_sem.at[peer], recv_sem.at[me]
            ).start()

        @pl.when(me == peer)
        def _():
            pltpu.make_async_copy(part(peer), held.at[peer], local_sem).start()

    for peer in range(groups):

        @pl.when(me != peer)
        def _():
            remote_copy(
                peer, part(peer), held.at[me], send_sem.at[peer], recv_sem.at[me]
            ).wait_send()
            remote_copy(
                peer, held.at[peer], held.at[peer], send_sem.at[peer], recv_sem.at[peer]
            ).wait_recv()

        @pl.when(me == peer)
        def _():
            pltpu.make_async_copy(part(peer), held.at[peer], local_sem).wait()

    def place(j, carry):
        group, slot, frame = item_place(index_ref[j], n_slots)
        out_ref[j] = held[group, slot, frame]
        return carry

    lax.fori_loop(0, out_ref.shape[0], place, 0)


def collect_kernel(
    groups, n_slots, index_ref, items_ref, out_ref, staged, send_sem, recv_sem, local_sem
):
    me = lax.axis_index("stream")
    greet_peers(groups, me)
    per_group = 2 * n_slots

    for peer in range(groups):

        def place(j, carry):
            group, slot, frame = item_place(j, n_slots)
            staged[group, slot, frame] = items_ref[index_ref[j]]
            return carry

        lax.fori_loop(peer * per_group, (peer + 1) * per_group, place, 0)

        @pl.when(me != peer)
        def _():
            remote_copy(
                peer, staged.at[peer], out_ref.at[me], send_sem.at[peer], recv_sem.at[me]
            ).start()

        @pl.when(me == peer)
        def _():
            pltpu.make_async_copy(staged.at[peer], out_ref.at[peer], local_sem).start()

    for peer in range(groups):

        @pl.when(me != peer)
        def _():
            remote_copy(
                peer, staged.at[peer], out_ref.at[me], send_sem.at[peer], recv_sem.at[me]
            ).wait_send()
            remote_copy(
                peer, out_ref.at[peer], out_ref.at[peer], send_sem.at[peer], recv_sem.at[peer]
            ).wait_recv()

        @pl.when(me == peer)
        def _():
            pltpu.make_async_copy(staged.at[peer], out_ref.at[peer], local_sem).wait()


def exchange(kernel, in_specs, out_spec, out_shape, block_shape, collective_id, args):
    groups, n_slots = block_shape[:2]
    return pl.pallas_call(
        functools.partial(kernel, groups, n_slots),
        out_shape=jax.ShapeDtypeStruct(out_shape, BF16),
        in_specs=in_specs,
        out_specs=out_spec,
        scratch_shapes=[
            pltpu.VMEM(block_shape, BF16),
            pltpu.SemaphoreType.DMA((groups,)),
            pltpu.SemaphoreType.DMA((groups,)),
            pltpu.SemaphoreType.DMA,
        ],
        compiler_params=pltpu.CompilerParams(
            collective_id=collective_id, has_side_effects=True, vmem_limit_bytes=VMEM_BYTES
        ),
    )(*args)


def gather_kernel(index_ref, source, out):
    def place(j, carry):
        out[j] = source[index_ref[j]]
        return carry

    lax.fori_loop(0, out.shape[0], place, 0)


def gather_items(source, index):
    return pl.pallas_call(
        gather_kernel,
        out_shape=jax.ShapeDtypeStruct(index.shape + source.shape[1:], source.dtype),
        in_specs=[SMEM, VMEM],
        out_specs=VMEM,
        compiler_params=pltpu.CompilerParams(vmem_limit_bytes=VMEM_BYTES),
    )(index, source)


def weight_copies(w_ref, w_s, sems, channels, dy):
    return [
        pltpu.make_async_copy(
            w_ref.at[t, dy, dx],
            w_s.at[dy, pl.ds(t * channels, channels), pl.ds(dx * channels, channels)],
            sems.at[t * 9 + dy * 3 + dx],
        )
        for t in range(3)
        for dx in range(3)
    ]


def start_weights(w_ref, w_s, sems, channels):
    @pl.when(pl.program_id(0) == 0)
    def _():
        for dy in range(3):
            for copy in weight_copies(w_ref, w_s, sems, channels, dy):
                copy.start()


def activate(values, gain):
    scaled = values * lax.rsqrt(jnp.mean(values * values, axis=-1, keepdims=True) + 1e-06)
    u = scaled * gain
    return u / (1.0 + jnp.exp(-u))


def conv_rows(x, w_ref, w_s, sems, cols, channels):
    rows = x.shape[0]
    col = lax.broadcasted_iota(jnp.int32, (rows, channels), 0) % cols
    sums = []
    for dy in range(3):

        @pl.when(pl.program_id(0) == 0)
        def _():
            for copy in weight_copies(w_ref, w_s, sems, channels, dy):
                copy.wait()

        r = jnp.dot(x, w_s[dy], preferred_element_type=F32)
        part = [r[:, dx * channels : (dx + 1) * channels] for dx in range(3)]
        left = jnp.where(col == 0, 0.0, pltpu.roll(part[0], 1, 0))
        right = jnp.where(col == cols - 1, 0.0, pltpu.roll(part[2], rows - 1, 0))
        sums.append((part[1] + left + right).reshape(-1, 2, cols, channels))
    return sums


def stack_times(count_ref, first_slot, kept, act):
    rows_out = []
    newer = []
    for s in range(act.shape[0]):
        done = count_ref[first_slot + s]
        older_on = done >= 2
        newer_on = done >= 1
        for y in range(2):
            old = kept[y, s, 0]
            new = kept[y, s, 1]
            old = jnp.where(older_on, old, jnp.zeros_like(old))
            new = jnp.where(newer_on, new, jnp.zeros_like(new))
            newer.append((s, y, new))
            rows_out.append(jnp.concatenate([old, new, act[s, y]], axis=-1))
    return jnp.concatenate(rows_out, axis=0), newer


def write_layer(sums, newer, act, part_ref, edge_ref, next_ref, extra):
    below, same, above = sums[0], sums[1], sums[2]
    part_ref[:, 0] = same[:, 0] + above[:, 1] + extra[:, 0]
    part_ref[:, 1] = same[:, 1] + below[:, 0] + extra[:, 1]
    edge_ref[0] = above[:, 0].astype(BF16)
    edge_ref[1] = below[:, 1].astype(BF16)
    for s, y, new in newer:
        next_ref[s, 0, y] = new
    next_ref[:, 1] = act


def first_kernel(
    cols, channels, count_ref, frame_ref, kept_ref, gain_ref, bias_ref, w_ref,
    part_ref, edge_ref, next_ref, w_s, sems,
):
    step = pl.program_id(0)

    start_weights(w_ref, w_s, sems, channels)

    act = activate(frame_ref[...].astype(F32), gain_ref[...]).astype(BF16)
    x, newer = stack_times(count_ref, step * act.shape[0], kept_ref[...], act)
    sums = conv_rows(x, w_ref, w_s, sems, cols, channels)
    extra = jnp.broadcast_to(bias_ref[...], act.shape)
    write_layer(sums, newer, act, part_ref, edge_ref, next_ref, extra)


def second_kernel(
    cols, channels, count_ref, up_ref, down_ref, frame_ref, kept_ref, gain_ref, bias_ref,
    hidden_ref, got_above_ref, got_below_ref, w_ref, part_ref, edge_ref, next_ref, w_s, sems,
):
    step = pl.program_id(0)

    start_weights(w_ref, w_s, sems, channels)

    slots = hidden_ref.shape[0]
    acts = []
    for s in range(slots):
        here = step * slots + s
        above = got_above_ref[s].astype(F32)
        below = got_below_ref[s].astype(F32)
        above = jnp.where(up_ref[here] > 0, above, 0.0)
        below = jnp.where(down_ref[here] > 0, below, 0.0)
        hidden = jnp.stack([hidden_ref[s, 0] + above, hidden_ref[s, 1] + below])
        acts.append(activate(hidden, gain_ref[...]).astype(BF16))
    act = jnp.stack(acts)
    x, newer = stack_times(count_ref, step * slots, kept_ref[...], act)
    sums = conv_rows(x, w_ref, w_s, sems, cols, channels)
    extra = frame_ref[...].astype(F32) + bias_ref[...]
    write_layer(sums, newer, act, part_ref, edge_ref, next_ref, extra)


def layer_specs(layer, n_slots, cols, channels):
    step = SLOTS_PER_STEP
    frame = pl.BlockSpec((step, 2, cols, channels), lambda i: (i, 0, 0, 0))
    kept = pl.BlockSpec(
        (2, step, 2, cols, channels), lambda i, layer=layer: (layer, i, 0, 0, 0)
    )
    vector = pl.BlockSpec((1, channels), lambda i: (0, 0))
    edge = pl.BlockSpec((step, cols, channels), lambda i: (i, 0, 0))
    outs = [
        pl.BlockSpec((step, 2, cols, channels), lambda i: (i, 0, 0, 0)),
        pl.BlockSpec((2, step, cols, channels), lambda i: (0, i, 0, 0)),
        pl.BlockSpec((step, 2, 2, cols, channels), lambda i: (i, 0, 0, 0, 0)),
    ]
    shapes = [
        jax.ShapeDtypeStruct((n_slots, 2, cols, channels), F32),
        jax.ShapeDtypeStruct((2, n_slots, cols, channels), BF16),
        jax.ShapeDtypeStruct((n_slots, 2, 2, cols, channels), BF16),
    ]
    scratch = [
        pltpu.VMEM((3, 3 * channels, 3 * channels), BF16),
        pltpu.SemaphoreType.DMA((27,)),
    ]
    return frame, kept, vector, edge, outs, shapes, scratch


def layer_call(kernel, in_specs, outs, shapes, scratch, n_slots, cols, channels, args):
    flops = 2 * n_slots * 2 * cols * 27 * channels * channels
    return pl.pallas_call(
        functools.partial(kernel, cols, channels),
        grid=(n_slots // SLOTS_PER_STEP,),
        in_specs=in_specs,
        out_specs=outs,
        out_shape=shapes,
        scratch_shapes=scratch,
        compiler_params=pltpu.CompilerParams(
            dimension_semantics=("arbitrary",), vmem_limit_bytes=VMEM_BYTES
        ),
        cost_estimate=pl.CostEstimate(
            flops=flops, bytes_accessed=27 * channels * channels * 2 + 8 * 2**20, transcendentals=0
        ),
    )(*args)


def trade_edges(edges):
    n = lax.axis_size("tile")
    from_below = lax.ppermute(edges[0], "tile", [((i + 1) % n, i) for i in range(n)])
    from_above = lax.ppermute(edges[1], "tile", [(i, (i + 1) % n) for i in range(n)])
    return from_above, from_below


def rotate_lots(buffer, starts, counts, places, scale):
    n = lax.axis_size("tile")
    room = buffer.shape[0]
    mirrored = jnp.concatenate([counts[:1], counts[1:][::-1]])
    largest = jnp.maximum(counts, mirrored)
    sizes = jnp.array(LOT_SIZES[:-1], jnp.int32)
    lots = jnp.sum((largest[:, None] > sizes[None, :]).astype(jnp.int32), axis=1)
    for digit in range(1, places // 2 + 1):
        turns = sorted({digit, places - digit})

        def branch(size, buffer, starts, counts, turns=turns):
            if size == 0:
                return buffer
            moved = []
            for turn in turns:
                pairs = [(i, (i + turn * scale) % n) for i in range(n)]
                at = jnp.minimum(starts[turn], room - size)
                lot = lax.dynamic_slice_in_dim(buffer, at, size, axis=0)
                moved.append((turn, at, lax.ppermute(lot, "tile", pairs)))
            for turn, at, values in moved:
                spot = at + jnp.arange(size, dtype=jnp.int32)
                taken = (spot >= starts[turn]) & (spot < starts[turn] + counts[turn])
                kept = lax.dynamic_slice_in_dim(buffer, at, size, axis=0)
                kept = jnp.where(taken[:, None, None], values, kept)
                buffer = lax.dynamic_update_slice_in_dim(buffer, kept, at, axis=0)
            return buffer

        buffer = lax.switch(
            lots[digit],
            [functools.partial(branch, size) for size in LOT_SIZES],
            buffer,
            starts,
            counts,
        )
    return buffer


def lookup(held_table, values):
    return jnp.sum(jnp.where(held_table, values[None, :], 0), axis=1)


def local(
    frame_in,
    cache_first,
    cache_second,
    gain_first,
    gain_second,
    conv_first,
    conv_second,
    bias_first,
    bias_second,
    old_slot,
    new_slot,
    old_shift,
    new_shift,
    frame_count,
):
    n_slots, n_rows, cols, channels = frame_in.shape
    groups = lax.axis_size("stream")
    n_tiles = lax.axis_size("tile")
    my_group = lax.axis_index("stream")
    my_tile = lax.axis_index("tile")
    flight = old_slot.shape[0]
    ids = jnp.arange(flight, dtype=jnp.int32)
    held_old = old_slot[None, :] == ids[:, None]
    held_new = new_slot[None, :] == ids[:, None]
    turn = (new_shift - old_shift) % n_tiles
    item_turn = lookup(held_old, turn)
    item_done = lookup(held_old, frame_count)
    live = jnp.stack([item_done >= 2, item_done >= 1], axis=1).reshape(-1)
    item_turn = jnp.where(live, jnp.repeat(item_turn, 2), 0)
    n_items = 2 * flight
    item_ids = jnp.arange(n_items, dtype=jnp.int32)

    block_shape = (groups, n_slots, 2, cols, channels)
    buffer = None
    position = item_ids
    scale = 1
    while scale < n_tiles:
        places = min(8, n_tiles // scale)
        digit = item_turn // scale % places
        rank_key = jnp.where(digit == 0, places, digit)
        ahead = (rank_key[None, :] < rank_key[:, None]) | (
            (rank_key[None, :] == rank_key[:, None]) & (item_ids[None, :] < item_ids[:, None])
        )
        new_position = jnp.sum(ahead.astype(jnp.int32), axis=1)
        digits = jnp.arange(places, dtype=jnp.int32)
        counts = jnp.sum((digit[None, :] == digits[:, None]).astype(jnp.int32), axis=1)
        before = (rank_key[None, :] < digits[:, None]).astype(jnp.int32)
        starts = jnp.sum(before, axis=1)
        index = jnp.sum(
            jnp.where(new_position[None, :] == item_ids[:, None], position[None, :], 0), axis=1
        )
        if buffer is None:
            buffer = exchange(
                spread_kernel,
                [SMEM, ANY, ANY],
                VMEM,
                (n_items, cols, channels),
                block_shape,
                0,
                (index, cache_first, cache_second),
            )
        else:
            buffer = gather_items(buffer, index)
        buffer = rotate_lots(buffer, starts, counts, places, scale)
        position = new_position
        scale *= places

    origin = lookup(held_new, old_slot)
    wanted = (origin[:, None] * 2 + jnp.arange(2, dtype=jnp.int32)[None, :]).reshape(-1)
    final = jnp.sum(
        jnp.where(wanted[:, None] == item_ids[None, :], position[None, :], 0), axis=1
    )
    kept = exchange(
        collect_kernel, [SMEM, VMEM], ANY, block_shape, block_shape, 1, (final, buffer)
    )

    begin = my_group * n_slots
    my_count = lax.dynamic_slice_in_dim(lookup(held_new, frame_count), begin, n_slots)
    my_shift = lax.dynamic_slice_in_dim(lookup(held_new, new_shift), begin, n_slots)
    number = (my_tile - my_shift) % n_tiles
    has_above = (number != 0).astype(jnp.int32)
    has_below = (number != n_tiles - 1).astype(jnp.int32)

    gain_first, gain_second = gain_first.reshape(1, -1), gain_second.reshape(1, -1)
    bias_first, bias_second = bias_first.reshape(1, -1), bias_second.reshape(1, -1)
    frame, kept_spec, vector, edge, outs, shapes, scratch = layer_specs(0, n_slots, cols, channels)
    hidden, edges, next_first = layer_call(
        first_kernel,
        [SMEM, frame, kept_spec, vector, vector, ANY],
        outs, shapes, scratch, n_slots, cols, channels,
        (my_count, frame_in, kept, gain_first, bias_first, conv_first),
    )
    from_above, from_below = trade_edges(edges)
    frame, kept_spec, vector, edge, outs, shapes, scratch = layer_specs(1, n_slots, cols, channels)
    second, edges, next_second = layer_call(
        second_kernel,
        [SMEM, SMEM, SMEM, frame, kept_spec, vector, vector, frame, edge, edge, ANY],
        outs, shapes, scratch, n_slots, cols, channels,
        (
            my_count, has_above, has_below, frame_in, kept, gain_second, bias_second,
            hidden, from_above, from_below, conv_second,
        ),
    )
    from_above, from_below = trade_edges(edges)
    above_on = has_above[:, None, None] > 0
    below_on = has_below[:, None, None] > 0
    mixed_frame = jnp.stack(
        [
            second[:, 0] + jnp.where(above_on, from_above.astype(F32), 0.0),
            second[:, 1] + jnp.where(below_on, from_below.astype(F32), 0.0),
        ],
        axis=1,
    ).astype(BF16)
    return (mixed_frame, next_first, next_second)


def solution(mesh):
    whole = (
        P("stream", "tile", None, None),
        P("stream", None, "tile", None, None),
        P("stream", None, "tile", None, None),
    )
    return jax.shard_map(
        local,
        mesh=mesh,
        in_specs=whole + (P(),) * 11,
        out_specs=whole,
        check_vma=False,
    )
```
